32 devices in a mesh: prow: 4 (over y, x), pcol: 8 (over z, core).
Axes of the slice: x: 2, y: 2, z: 4, core: 2. Of those that a mesh axis runs over, the one named last changes fastest.
Arguments:
- covariance: float32 [4, 16, 256, 8, 8, 256], P('prow', None, None, 'pcol'), may hold values from 0 to 3, as said below
Outputs:
- factored: float32 [4, 16, 256, 8, 8, 256], P('prow', None, None, 'pcol')
The draws below stay inside these ranges and needn't reach their ends.
Inputs may be any that keep to these rules, and one draw needn't show every extreme that they name: covariance is symmetric and positive definite.
All inputs are finite; a program needn't handle non-finite values.
Results may differ from the reference program's by a relative error of at most 0.0003.
Values sent between devices are 32-bit elements; how exact they have to be, the bound alone decides.
A program may use at most 192 MiB of HBM per device.

```python
import jax
import jax.numpy as jnp
from jax import lax

N = 16384
NB = 256
PANELS = 2
RT = 16
CT = 8
N_PROW = 4
N_PCOL = 8


def draw_covariance(key, part):
    key_points, key_scale, key_nugget = jax.random.split(jax.random.fold_in(key, 71), 3)
    points = jax.random.uniform(key_points, (N, 6), jnp.float32)
    spread = jax.random.uniform(key_scale, (N,), jnp.float32, 0.6, 1.5)
    nugget = jax.random.uniform(key_nugget, (N,), jnp.float32, 0.2, 0.6)
    row_pts = points.reshape(RT, N_PROW, NB, 6).transpose(1, 0, 2, 3)
    col_pts = points.reshape(CT, N_PCOL, NB, 6).transpose(1, 0, 2, 3)
    squared = jnp.zeros((N_PROW, RT, NB, N_PCOL, CT, NB), jnp.float32)
    for coord in range(6):
        diff = row_pts[:, :, :, coord][:, :, :, None, None, None] - col_pts[:, :, :, coord][None, None, None]
        squared = squared + diff * diff
    scaled = jnp.sqrt(squared) * 3.0 ** 0.5
    kernel = (1.0 + scaled) * jnp.exp(-scaled)
    row_spread = spread.reshape(RT, N_PROW, NB).transpose(1, 0, 2)[:, :, :, None, None, None]
    col_spread = spread.reshape(CT, N_PCOL, NB).transpose(1, 0, 2)[None, None, None]
    row_ids = jnp.arange(N, dtype=jnp.int32).reshape(RT, N_PROW, NB).transpose(1, 0, 2)[:, :, :, None, None, None]
    col_ids = jnp.arange(N, dtype=jnp.int32).reshape(CT, N_PCOL, NB).transpose(1, 0, 2)[None, None, None]
    row_nugget = nugget.reshape(RT, N_PROW, NB).transpose(1, 0, 2)[:, :, :, None, None, None]
    return row_spread * col_spread * kernel + jnp.where(row_ids == col_ids, row_nugget, 0.0)


def setup_inputs(seed: int = 0) -> dict:
    splits = jax.random.split(jax.random.key(seed), 2)
    covariance = draw_covariance(jax.random.fold_in(splits[1], 71), 0)
    return {"covariance": covariance}


def to_full(tiles):
    return tiles.transpose(1, 0, 2, 4, 3, 5).reshape(N, N)

def to_tiles(full):
    return full.reshape(RT, N_PROW, NB, CT, N_PCOL, NB).transpose(1, 0, 2, 4, 3, 5)

def reference(covariance):
    full = to_full(covariance)
    for panel in range(PANELS):
        lower = panel * NB
        upper = lower + NB
        factor = jnp.linalg.cholesky(full[lower:upper, lower:upper])
        below = jax.scipy.linalg.solve_triangular(factor, full[upper:, lower:upper].T, lower=True).T
        update = jnp.dot(below, below.T, precision=lax.Precision.HIGHEST)
        full = full.at[upper:, upper:].add(-update)
        full = full.at[lower:upper, lower:upper].set(factor)
        full = full.at[upper:, lower:upper].set(below)
        full = full.at[lower:upper, upper:].set(jnp.zeros((NB, N - upper), jnp.float32))
    return to_tiles(full)
```

```python
import jax
import jax.numpy as jnp
from jax import lax
from jax.experimental import pallas as pl
from jax.experimental.pallas import tpu as pltpu
from jax.sharding import PartitionSpec as P

PANELS = 2
CHUNKS = 8
HIGHEST = lax.Precision.HIGHEST


def rows_along_pcol(own, pcols, pcol_at):
    pairs = pcols // 2
    pair_at = pcol_at // 2
    perm = [(q, q + 2) for q in range(pcols - 2)]
    size = own.shape[0] // CHUNKS
    chunks = own.reshape((CHUNKS, size) + own.shape[1:])
    got = []
    for slot in range(CHUNKS + pairs - 2):
        first = chunks[min(slot, CHUNKS - 1)]
        send = first if slot == 0 else jnp.where(pair_at == 0, first, got[-1])
        got.append(lax.ppermute(send, "pcol", perm))
    stacked = jnp.stack(got)
    here = lax.dynamic_slice_in_dim(stacked, jnp.maximum(pair_at - 1, 0), CHUNKS, 0)
    mine = jnp.where(pair_at == 0, chunks, here).reshape(own.shape)
    other = lax.ppermute(mine, "pcol", [(q, q ^ 1) for q in range(pcols)])
    even = pcol_at % 2 == 0
    return jnp.where(even, mine, other), jnp.where(even, other, mine)


def cols_along_prow(own, prows, prow_at):
    mine = own
    width = 2
    while width < prows:
        got = lax.ppermute(mine, "prow", [(p, p + width) for p in range(width)])
        mine = jnp.where((prow_at >= width) & (prow_at < 2 * width), got, mine)
        width *= 2
    other = lax.ppermute(mine, "prow", [(p, p ^ 1) for p in range(prows)])
    even = prow_at % 2 == 0
    return jnp.concatenate([jnp.where(even, mine, other), jnp.where(even, other, mine)], 0)


def split(value):
    high = value.astype(jnp.bfloat16)
    low = (value - high.astype(jnp.float32)).astype(jnp.bfloat16)
    return high, low


def update_kernel(place, tiles_ref, rows_ref, cols_ref, out_ref, rows_all, cols_all):
    step = pl.program_id(0)
    depth = cols_ref.shape[0]
    count = tiles_ref.shape[2]
    tile = tiles_ref.shape[3]

    @pl.when(step == 0)
    def _():
        for c in range(count):
            at = pl.ds(c * tile, tile)
            high, low = split(cols_ref[:, at])
            cols_all[pl.ds(0, depth), at] = high
            cols_all[pl.ds(depth, depth), at] = low
            cols_all[pl.ds(2 * depth, depth), at] = high

    high, low = split(rows_ref[0])
    rows_all[:, pl.ds(0, depth)] = high
    rows_all[:, pl.ds(depth, depth)] = high
    rows_all[:, pl.ds(2 * depth, depth)] = low
    top = step * place[2] + place[0] < PANELS
    panel = place[1]
    for c in range(count):
        term = jnp.dot(
            rows_all[...], cols_all[:, pl.ds(c * tile, tile)], preferred_element_type=jnp.float32
        )
        value = jnp.where(top, 0.0, tiles_ref[0, :, c, :] - term)
        if c == 0:
            value = jnp.where(panel == 0, rows_ref[0, :, pl.ds(0, tile)], value)
            value = jnp.where(panel == 1, rows_ref[0, :, pl.ds(tile, tile)], value)
        out_ref[0, :, c, :] = value


def update(place, tiles, rows_term, cols_term):
    rt_count, tile, ct_count, _ = tiles.shape
    depth = cols_term.shape[0]
    block = pl.BlockSpec((1, tile, ct_count, tile), lambda r, place: (r, 0, 0, 0))
    size = 2 * tiles.size * 4
    return pl.pallas_call(
        update_kernel,
        grid_spec=pltpu.PrefetchScalarGridSpec(
            num_scalar_prefetch=1,
            grid=(rt_count,),
            in_specs=[
                block,
                pl.BlockSpec((1, tile, depth), lambda r, place: (r, 0, 0)),
                pl.BlockSpec((depth, ct_count * tile), lambda r, place: (0, 0)),
            ],
            out_specs=block,
            scratch_shapes=[
                pltpu.VMEM((tile, 3 * depth), jnp.bfloat16),
                pltpu.VMEM((3 * depth, ct_count * tile), jnp.bfloat16),
            ],
        ),
        out_shape=jax.ShapeDtypeStruct(tiles.shape, jnp.float32),
        compiler_params=pltpu.CompilerParams(vmem_limit_bytes=48 * 1024 * 1024),
        cost_estimate=pl.CostEstimate(
            flops=6 * depth * tiles.size, bytes_accessed=size, transcendentals=0
        ),
    )(place, tiles, rows_term, cols_term)


def per_device(covariance):
    prows = lax.axis_size("prow")
    pcols = lax.axis_size("pcol")
    prow_at = lax.axis_index("prow")
    pcol_at = lax.axis_index("pcol")
    rt_count = covariance.shape[1]
    tile = covariance.shape[2]
    ct_count = covariance.shape[4]
    tiles = covariance.reshape(rt_count, tile, ct_count, tile)

    corner = tiles[0, :, 0, :]
    inside = (prow_at < PANELS) & (pcol_at < PANELS)
    spots = [
        jnp.where(inside & (prow_at == i) & (pcol_at == j), corner, 0.0)
        for i, j in ((0, 0), (1, 0), (1, 1))
    ]
    a00, a10, a11 = lax.psum(jnp.stack(spots), ("prow", "pcol"))

    raw_cols = cols_along_prow(tiles[0].reshape(tile, ct_count * tile), prows, prow_at)
    raw_0, raw_1 = rows_along_pcol(tiles[:, :, 0, :].reshape(rt_count * tile, tile), pcols, pcol_at)

    eye = jnp.eye(tile, dtype=jnp.float32)
    l00 = jnp.linalg.cholesky(a00, symmetrize_input=False)
    i00 = jax.scipy.linalg.solve_triangular(l00, eye, lower=True)
    l10 = jnp.dot(a10, i00.T, precision=HIGHEST)
    l11 = jnp.linalg.cholesky(a11 - jnp.dot(l10, l10.T, precision=HIGHEST), symmetrize_input=False)
    i11 = jax.scipy.linalg.solve_triangular(l11, eye, lower=True)

    def solve(first, second):
        one = jnp.dot(first, i00.T, precision=HIGHEST)
        two = jnp.dot(second - jnp.dot(one, l10.T, precision=HIGHEST), i11.T, precision=HIGHEST)
        return one, two

    rows_0, rows_1 = solve(raw_0, raw_1)
    top = jnp.dot(i00, raw_cols[:tile], precision=HIGHEST)
    low = jnp.dot(
        i11, raw_cols[tile:] - jnp.dot(l10, top, precision=HIGHEST), precision=HIGHEST
    )
    cols_term = jnp.concatenate([top, low], 0)
    rows_term = jnp.concatenate([rows_0, rows_1], 1).reshape(rt_count, tile, 2 * tile)
    row_index = (jnp.arange(rt_count, dtype=jnp.int32) * prows + prow_at)[:, None, None]
    d0 = jnp.concatenate([l00, jnp.zeros_like(l00)], 1)
    d1 = jnp.concatenate([l10, l11], 1)
    rows_term = jnp.where(row_index == 0, d0, jnp.where(row_index == 1, d1, rows_term))

    place = jnp.stack([prow_at, pcol_at, jnp.int32(prows)]).astype(jnp.int32)
    out = update(place, tiles, rows_term, cols_term)
    return out.reshape(1, rt_count, tile, 1, ct_count, tile)


def solution(mesh):
    return jax.shard_map(
        per_device,
        mesh=mesh,
        in_specs=(P("prow", None, None, "pcol", None, None),),
        out_specs=P("prow", None, None, "pcol", None, None),
        check_vma=False,
    )
```
